32 devices in a mesh: dp: 4 (over x, core), expert: 8 (over z, y).
Axes of the slice: x: 2, y: 2, z: 4, core: 2. Of those that a mesh axis runs over, the one named last changes fastest.
Arguments:
- tokens: bfloat16 [4, 1024, 4096], P('dp', 'expert'), may hold values from -6 to 6
- norm_gain: float32 [4096], replicated, may hold values from 0.5 to 1.5
- router_weight: float32 [8, 4096], replicated, may hold values from -0.09375 to 0.09375
- value_weight: float32 [4096], replicated, may hold values from -0.09375 to 0.09375
- gate_weight: bfloat16 [8, 1536, 4096], P('expert', 'dp'), may hold values from -0.09375 to 0.09375
- up_weight: bfloat16 [8, 1536, 4096], P('expert', 'dp'), may hold values from -0.09375 to 0.09375
- down_weight: bfloat16 [8, 1536, 4096], P('expert', 'dp'), may hold values from -0.15625 to 0.15625
- routes: int32 [4, 1024, 2], P('dp', 'expert'), may hold values from 0 to 7, all different within a row; in each aligned block of 128 rows (0 to 127, 128 to 255, ..., all dimensions but the last counted through in order) at most 48 rows name the same one
- segment_ids: int32 [4, 1024], P('dp', 'expert'), may hold values from 0 to 7, never falling along the last dimension, each value on 1 to 256 neighbouring positions
- loss_mask: int32 [4, 1024], P('dp', 'expert'), may hold values 0 or 1
- penalty_reward: float32 [4, 1024], P('dp', 'expert'), may hold values from -0.3 to 0.3
- scores: float32 [4, 8], P('dp'), may hold values from -6 to 6
Outputs:
- values: float32 [4, 1024], P('dp', 'expert')
- mean_loss: float32 [], replicated
- value_grad: float32 [4096], replicated
- router_grad: float32 [8, 4096], replicated
- gate_grad: bfloat16 [8, 1536, 4096], P('expert', 'dp')
- up_grad: bfloat16 [8, 1536, 4096], P('expert', 'dp')
- down_grad: bfloat16 [8, 1536, 4096], P('expert', 'dp')
The draws below stay inside these ranges and needn't reach their ends.
Inputs may be any that keep to these rules, and one draw needn't show every extreme that they name: Each token names 2 different experts; within the tokens of one device no expert is named by more than 48 routes, a bound that some block reaches. `segment_ids`: within each data row the ids never fall; each response holds 1 to 256 tokens and one holds exactly 256.
All inputs are finite; a program needn't handle non-finite values. No bound on the sum of `loss_mask` on one device may be relied on, other than what follows from the above.
Results may differ from the reference program's by a relative error of at most 0.0069.
Values may be sent and summed in bfloat16 or wider, within the bound.
A program may use at most 192 MiB of HBM per device.

```python
import functools
import math
import jax
import jax.numpy as jnp
import numpy as np
from jax import lax

D = 4096
FF = 1536
TOPK = 2
SEGS = 8
TOK_DEV = 128
EXPERTS = 8
ROW_TOK = 1024
MOST = 256
CAP = 48
N_DP = 4
N_EXPERT = 8


def plant(array, stream_key, low, top_value):
    place = [jax.random.randint(jax.random.fold_in(stream_key, axis), (), 0, length) for axis, length in enumerate(array.shape)]
    widest = array.shape.index(max(array.shape))
    next_to = place[:widest] + [(place[widest] + 1) % array.shape[widest]] + place[widest + 1:]
    return array.at[tuple(place)].set(low).at[tuple(next_to)].set(top_value)


def shard_levels(key, shape, split, least, high):
    gain, own = 1.0, jax.random.fold_in(key, 6)
    for axis_at, shards_of in split:
        draws = jnp.exp(jax.random.uniform(jax.random.fold_in(own, axis_at), (shards_of,), jnp.float32, least / len(split), high / len(split)))
        gain = gain * jnp.repeat(draws, shape[axis_at] // shards_of).reshape([-1 if axis == axis_at else 1 for axis in range(len(shape))])
    return gain


def split_up(number_of, total, bound, slope):
    loads = [(1 << 20) // math.isqrt(standing ** slope) + 1 for standing in range(2, number_of + 1)]
    rest, given = total - bound - (number_of - 1), [1] * (number_of - 1)
    while rest > 0:
        candidates = [i for i in range(number_of - 1) if given[i] < bound]
        pool, left = sum([loads[i] for i in candidates]), rest
        for i in candidates:
            extra = min(bound - given[i], max(1, left * loads[i] // pool), rest)
            given[i] = given[i] + extra
            rest = rest - extra
    return np.array([bound] + given)


def ragged(rng, count, total, bound, slope):
    if count == 2:
        one = jax.random.randint(rng, (), max(1, total - bound), min(bound, total - 1) + 1)
        return jnp.stack([one, total - one])
    sizes = jnp.asarray(split_up(count, total, bound, slope), jnp.int32)
    twos = (count - 1) // 2
    giver, receiver = sizes[1:1 + 2 * twos:2], sizes[2:2 + 2 * twos:2]
    room = jnp.minimum(giver - 1, bound - receiver)
    shifted = jax.random.randint(jax.random.fold_in(rng, 1), (twos,), 0, 1 << 20) % (room + 1)
    sizes = sizes.at[1:1 + 2 * twos:2].set(giver - shifted).at[2:2 + 2 * twos:2].set(receiver + shifted)
    return sizes[jax.random.permutation(jax.random.fold_in(rng, 2), count)]


def shared_out(key, own, number, rows, amount, top, reach, slope):
    ranking = jax.random.permutation(key, amount)
    packed, ordinary = load_shares(amount, rows * top, reach, slope, True), load_shares(amount, rows * top, reach, slope, False)
    places = jnp.arange(amount)

    def named(lengths, rotation):
        used = int((lengths > 0).sum())
        fixed = max(1, used // 4)
        passed = fixed + (places - fixed + rotation * (used - fixed)) % max(1, amount - fixed)
        return jnp.zeros((amount,), jnp.int32).at[ranking[jnp.where(places < fixed, places, passed)]].set(jnp.asarray(lengths, jnp.int32))

    lengths = jnp.where(number % 4 == 0, named(packed, number // 4), named(ordinary, number - number // 4 - 1))
    mixed = jax.random.permutation(jax.random.fold_in(own, 3), amount)
    giver, receiver = mixed[0:amount // 2 * 2:2], mixed[1:amount // 2 * 2:2]
    room = jnp.minimum(lengths[giver] - 1, reach - lengths[receiver]) // 2
    room = jnp.where((giver == ranking[0]) | (receiver == ranking[0]) | (lengths[receiver] == 0), 0, jnp.maximum(room, 0))
    passed = jax.random.randint(jax.random.fold_in(own, 4), (amount // 2,), 0, 1 << 20) % (room + 1)
    lengths = lengths.at[giver].add(-passed).at[receiver].add(passed)
    members = jnp.searchsorted(jnp.cumsum(lengths), jnp.arange(rows * top), side="right").astype(jnp.int32)
    grid = members.reshape(top, rows).T
    grid = grid[jax.random.permutation(jax.random.fold_in(own, 1), rows)]
    rotation = jax.random.randint(jax.random.fold_in(own, 2), (rows, 1), 0, top)
    return jnp.take_along_axis(grid, (jnp.arange(top)[None, :] + rotation) % top, axis=1)


def load_shares(count, total, reach, skew, full):
    loads = [(1 << 20) // math.isqrt(grade ** skew) + 1 for grade in range(1, count + 1)]
    largest = reach if full else min(reach, max(-(-total // count), total * loads[0] // sum(loads)))
    least = 1 if total - largest >= count - 1 else 0
    holding, surplus = [largest] + [least] * (count - 1), total - largest - least * (count - 1)
    while surplus > 0:
        movable = [i for i in range(1, count) if holding[i] < largest] or [i for i in range(1, count) if holding[i] < reach]
        whole, left = sum([loads[i] for i in movable]), surplus
        for i in movable:
            addition = min(reach - holding[i], max(1, left * loads[i] // whole), surplus)
            holding[i] = holding[i] + addition
            surplus = surplus - addition
    return np.array(holding)


def noise(key, shape, width, limit, split=(), kind=jnp.bfloat16):
    array = width * jax.random.normal(key, shape, jnp.float32)
    if split:
        array = array * shard_levels(key, shape, split, -0.22, 0.18)
    return jnp.clip(array, -limit, limit).astype(kind)


def setup_inputs(seed: int = 0) -> dict:
    arg_keys = jax.random.split(jax.random.key(seed), 13)
    tokens = noise(arg_keys[0], (N_DP, ROW_TOK, D), 1.0, 6.0, ((0, 4), (1, 8)))
    norm_gain = jnp.clip(1.0 + 0.1 * jax.random.normal(arg_keys[1], (D,), jnp.float32), 0.5, 1.5)
    router_weight = noise(arg_keys[2], (EXPERTS, D), D ** -0.5, 0.09375, (), jnp.float32)
    value_weight = noise(arg_keys[3], (D,), D ** -0.5, 0.09375, (), jnp.float32)
    gate_weight = noise(arg_keys[4], (EXPERTS, FF, D), D ** -0.5, 0.09375, ((0, 8), (1, 4)))
    up_weight = noise(arg_keys[5], (EXPERTS, FF, D), D ** -0.5, 0.09375, ((0, 8), (1, 4)))
    down_weight = noise(arg_keys[6], (EXPERTS, FF, D), FF ** -0.5, 0.15625, ((0, 8), (1, 4)))
    routes_keys = jax.random.split(jax.random.fold_in(arg_keys[7], 1), N_DP * ROW_TOK // TOK_DEV)
    routes_turns = jax.random.permutation(jax.random.fold_in(arg_keys[7], 3), N_DP * ROW_TOK // TOK_DEV)
    routes = jax.vmap(lambda own, number: shared_out(jax.random.fold_in(arg_keys[7], 2), own, number, TOK_DEV, EXPERTS, TOPK, CAP, 2))(routes_keys, routes_turns).reshape((N_DP, ROW_TOK, TOPK))
    segment_ids = jax.vmap(lambda own: jnp.searchsorted(jnp.cumsum(ragged(own, SEGS, ROW_TOK, MOST, 1)), jnp.arange(ROW_TOK), side="right"))(jax.random.split(arg_keys[8], N_DP)).reshape((N_DP, ROW_TOK)).astype(jnp.int32)
    loss_mask = plant((jax.random.randint(arg_keys[9], (N_DP, ROW_TOK), 0, 4) < 3).astype(jnp.int32), jax.random.fold_in(arg_keys[9], 1), 0, 1)
    penalty_reward = noise(arg_keys[10], (N_DP, ROW_TOK), 0.05, 0.3, ((0, 4), (1, 8)), jnp.float32)
    scores = noise(arg_keys[11], (N_DP, SEGS), 1.0, 6.0, ((0, 4),), jnp.float32)
    return dict(tokens=tokens, norm_gain=norm_gain, router_weight=router_weight, value_weight=value_weight, gate_weight=gate_weight, up_weight=up_weight, down_weight=down_weight, routes=routes, segment_ids=segment_ids, loss_mask=loss_mask, penalty_reward=penalty_reward, scores=scores)


discount_rate = 0.9995
norm_epsilon = 1e-06
white_epsilon = 1e-05
highest = lax.Precision.HIGHEST

def norm_rows(tokens, norm_gain):
    as_float = tokens.astype(jnp.float32)
    inverse_rms = lax.rsqrt(lax.optimization_barrier(jnp.mean(as_float * as_float, axis=-1, keepdims=True)) + norm_epsilon)
    return (as_float * inverse_rms * norm_gain).astype(jnp.bfloat16)

def slot_numbers(block_routes, experts):
    flattened = block_routes.reshape(-1)
    onehot = (flattened[:, None] == jnp.arange(experts, dtype=jnp.int32)[None, :]).astype(jnp.int32)
    before = jnp.cumsum(onehot, axis=0) - onehot
    return lax.optimization_barrier(jnp.sum(before * onehot, axis=1)).astype(jnp.int32).reshape(block_routes.shape)

def row_returns(reward, segment):
    following = jnp.concatenate([segment[1:], jnp.full((1,), -1, jnp.int32)])
    same_next = (following == segment).astype(jnp.float32)

    def backward_step(carry, item):
        reward_now, same = item
        result = reward_now + discount_rate * carry * same
        return (result, result)
    final_carry, result = lax.scan(backward_step, jnp.zeros((), jnp.float32), (reward, same_next), reverse=True)
    return result

def reference(tokens, norm_gain, router_weight, value_weight, gate_weight, up_weight, down_weight, routes, segment_ids, loss_mask, penalty_reward, scores):
    blocks = N_DP * N_EXPERT
    all_tokens = blocks * TOK_DEV
    flat_tokens = tokens.reshape(all_tokens, D)
    normed = norm_rows(flat_tokens, norm_gain)
    flat_routes = routes.reshape(all_tokens, TOPK)
    last_last = (((1,), (1,)), ((), ()))
    first_first = (((0,), (0,)), ((), ()))
    logits = lax.dot_general(normed.astype(jnp.float32), router_weight, last_last, precision=highest)
    chosen = jnp.take_along_axis(logits, flat_routes, axis=1)
    gate_sigmoid = jax.nn.sigmoid(chosen)
    sigmoid_total = lax.optimization_barrier(jnp.sum(gate_sigmoid, axis=1, keepdims=True))
    route_prob = gate_sigmoid / sigmoid_total
    slot_number = jax.vmap(functools.partial(slot_numbers, experts=EXPERTS))(flat_routes.reshape(blocks, TOK_DEV, TOPK)).reshape(all_tokens, TOPK)
    block_of = jnp.arange(all_tokens, dtype=jnp.int32) // TOK_DEV
    token_ids = jnp.broadcast_to(jnp.arange(all_tokens, dtype=jnp.int32)[:, None], (all_tokens, TOPK))
    slot_place = ((flat_routes * blocks + block_of[:, None]) * CAP + slot_number).reshape(-1)
    source_index = jnp.full((EXPERTS * blocks * CAP,), all_tokens, jnp.int32).at[slot_place].set(token_ids.reshape(-1))
    source_index = source_index.reshape(EXPERTS, blocks * CAP)
    padded = jnp.concatenate([normed, jnp.zeros((1, D), jnp.bfloat16)], axis=0)

    def forward_one(inputs):
        index_row, gate_mat, up_mat, down_mat = inputs
        expert_rows = padded[index_row]
        gate_value = lax.dot_general(expert_rows, gate_mat, last_last, preferred_element_type=jnp.float32)
        up_value = lax.dot_general(expert_rows, up_mat, last_last, preferred_element_type=jnp.float32)
        hidden = (gate_value * jax.nn.sigmoid(gate_value) * up_value).astype(jnp.bfloat16)
        value_along = jnp.dot(down_mat.astype(jnp.float32), value_weight, precision=highest)
        return (jnp.dot(hidden.astype(jnp.float32), value_along, precision=highest), gate_value, up_value)
    row_values, gate_all, up_all = lax.map(forward_one, (source_index, gate_weight, up_weight, down_weight))
    route_value = row_values.reshape(-1)[slot_place].reshape(all_tokens, TOPK)
    flat_values = jnp.dot(flat_tokens.astype(jnp.float32), value_weight, precision=highest) + lax.optimization_barrier(jnp.sum(route_prob * route_value, axis=1))
    values = flat_values.reshape(N_DP, ROW_TOK)
    following = jnp.concatenate([segment_ids[:, 1:], jnp.full((N_DP, 1), -1, jnp.int32)], axis=1)
    ending = following != segment_ids
    segment_hit = segment_ids[:, :, None] == jnp.arange(SEGS, dtype=jnp.int32)[None, None, :]
    score_pick = lax.optimization_barrier(jnp.sum(jnp.where(segment_hit, scores[:, None, :], 0.0), axis=2))
    reward = penalty_reward + jnp.where(ending, score_pick, 0.0)
    returns = jax.vmap(row_returns)(reward, segment_ids)
    mask_float = loss_mask.astype(jnp.float32)
    divisor = jnp.maximum(jnp.sum(mask_float), 1.0)
    centre = jnp.sum(mask_float * returns) / divisor
    variance = jnp.sum(mask_float * (returns - centre) * (returns - centre)) / divisor
    whitened = (returns - centre) * lax.rsqrt(variance + white_epsilon)
    value_error = mask_float * (values - whitened)
    mean_loss = 0.5 * jnp.sum(mask_float * (values - whitened) * (values - whitened)) / divisor
    flat_error = value_error.reshape(all_tokens)
    route_weight = flat_error[:, None] * route_prob
    prob_grad = flat_error[:, None] * route_value
    weight_table = jnp.zeros((EXPERTS * blocks * CAP,), jnp.float32).at[slot_place].set(route_weight.reshape(-1))
    weight_table = weight_table.reshape(EXPERTS, blocks * CAP)

    def backward_one(inputs):
        index_row, row_weight, gate_value, up_value, down_mat = inputs
        expert_rows = padded[index_row]
        gate_sig = jax.nn.sigmoid(gate_value)
        hidden = (gate_value * gate_sig * up_value).astype(jnp.bfloat16)
        down_float = down_mat.astype(jnp.float32)
        value_along = jnp.dot(down_float, value_weight, precision=highest)
        spread = jnp.dot(row_weight, hidden.astype(jnp.float32), precision=highest)
        down_part = (spread[:, None] * value_weight[None, :]).astype(jnp.bfloat16)
        hidden_grad = row_weight[:, None] * value_along[None, :]
        gate_delta = (hidden_grad * up_value * gate_sig * (1.0 + gate_value * (1.0 - gate_sig))).astype(jnp.bfloat16)
        up_delta = (hidden_grad * gate_value * gate_sig).astype(jnp.bfloat16)
        gate_part = lax.dot_general(gate_delta, expert_rows, first_first, preferred_element_type=jnp.float32).astype(jnp.bfloat16)
        up_part = lax.dot_general(up_delta, expert_rows, first_first, preferred_element_type=jnp.float32).astype(jnp.bfloat16)
        head_part = jnp.dot(spread, down_float, precision=highest)
        return (gate_part, up_part, down_part, head_part)
    gate_grad, up_grad, down_grad, head_parts = lax.map(backward_one, (source_index, weight_table, gate_all, up_all, down_weight))
    value_grad = jnp.dot(flat_error, flat_tokens.astype(jnp.float32), precision=highest) + lax.optimization_barrier(jnp.sum(head_parts, axis=0))
    sigma_grad = (prob_grad - lax.optimization_barrier(jnp.sum(prob_grad * route_prob, axis=1, keepdims=True))) / sigmoid_total
    chosen_grad = sigma_grad * gate_sigmoid * (1.0 - gate_sigmoid)
    expert_hit = flat_routes[:, :, None] == jnp.arange(EXPERTS, dtype=jnp.int32)[None, None, :]
    logit_grad = lax.optimization_barrier(jnp.sum(jnp.where(expert_hit, chosen_grad[:, :, None], 0.0), axis=1))
    router_grad = lax.dot_general(logit_grad, normed.astype(jnp.float32), first_first, precision=highest)
    return (values, mean_loss, value_grad, router_grad, gate_grad, up_grad, down_grad)
```

```python
import jax
import jax.numpy as jnp
from jax import lax
from jax.sharding import PartitionSpec as P

discount_rate = 0.9995
norm_epsilon = 1e-06
white_epsilon = 1e-05
highest = lax.Precision.HIGHEST


def passed_along(array, axis, by):
    size = lax.axis_size(axis)
    pairs = [(i, i + by) for i in range(size) if 0 <= i + by < size]
    return lax.ppermute(array, axis, pairs)


def entering(part, axis, combine, identity):
    count = lax.axis_size(axis)
    place = lax.axis_index(axis)
    ahead = count - 1 - place
    gathered = jax.tree.map(lambda a: lax.all_gather(a, axis), part)
    state = jax.tree.map(lambda a, e: jnp.zeros_like(a) + jnp.asarray(e, a.dtype), part, identity)

    def one(turn, state):
        source = count - 1 - turn
        return combine(
            state, jax.tree.map(lambda a: lax.dynamic_index_in_dim(a, source, 0, False), gathered)
        )

    return lax.fori_loop(0, ahead, one, state)


def norm_rows(tokens, norm_gain):
    as_float = tokens.astype(jnp.float32)
    inverse_rms = lax.rsqrt(jnp.mean(as_float * as_float, axis=-1, keepdims=True) + norm_epsilon)
    return (as_float * inverse_rms * norm_gain).astype(jnp.bfloat16)


def slot_numbers(block_routes, experts):
    flattened = block_routes.reshape(-1)
    place = jnp.arange(flattened.shape[0], dtype=jnp.int32)
    same = (flattened[:, None] == flattened[None, :]) & (place[None, :] < place[:, None])
    return jnp.sum(same.astype(jnp.int32), axis=1).reshape(block_routes.shape)


def compose(earlier, later):
    return (later[0] * earlier[0], later[1] + later[0] * earlier[1])


def shards(
    tokens,
    norm_gain,
    router_weight,
    value_weight,
    gate_weight,
    up_weight,
    down_weight,
    routes,
    segment_ids,
    loss_mask,
    penalty_reward,
    scores,
):
    tok_count = tokens.shape[1]
    model_width = tokens.shape[2]
    route_count = routes.shape[2]
    experts = router_weight.shape[0]
    hidden_width = gate_weight.shape[1]
    dp_count = lax.axis_size("dp")
    expert_count = lax.axis_size("expert")
    capacity = tok_count * route_count * 3 // (2 * experts)
    last_last = (((1,), (1,)), ((), ()))
    first_first = (((0,), (0,)), ((), ()))
    own_tokens = tokens[0]
    own_routes = routes[0]
    normed = norm_rows(own_tokens, norm_gain)
    logits = lax.dot_general(
        normed.astype(jnp.float32), router_weight, last_last, precision=highest
    )
    chosen = jnp.take_along_axis(logits, own_routes, axis=1)
    gate_sigmoid = jax.nn.sigmoid(chosen)
    sigmoid_total = jnp.sum(gate_sigmoid, axis=1, keepdims=True)
    route_prob = gate_sigmoid / sigmoid_total
    slot_number = slot_numbers(own_routes, experts)
    slot_place = (own_routes * capacity + slot_number).reshape(-1)
    token_ids = jnp.broadcast_to(jnp.arange(tok_count, dtype=jnp.int32)[:, None], own_routes.shape)
    source_index = (
        jnp.full((experts * capacity,), tok_count, jnp.int32)
        .at[slot_place]
        .set(token_ids.reshape(-1))
    )
    outgoing = jnp.take(normed, source_index, axis=0, mode="fill", fill_value=0).reshape(
        experts, capacity, model_width
    )
    incoming = lax.all_to_all(outgoing, "expert", split_axis=0, concat_axis=0, tiled=True)
    expert_rows = lax.all_gather(incoming[None], "dp", axis=0, tiled=True).reshape(-1, model_width)
    both_weights = jnp.concatenate([gate_weight[0], up_weight[0]], axis=0)
    both_values = lax.dot_general(
        expert_rows, both_weights, last_last, preferred_element_type=jnp.float32
    )
    gate_value = both_values[:, :hidden_width]
    up_value = both_values[:, hidden_width:]
    gate_sig = jax.nn.sigmoid(gate_value)
    hidden = (gate_value * gate_sig * up_value).astype(jnp.bfloat16)
    down_float = down_weight[0].astype(jnp.float32)
    value_along = jnp.dot(down_float, value_weight, precision=highest)
    partial_value = jnp.dot(hidden.astype(jnp.float32), value_along, precision=highest)
    partial_value = partial_value.reshape(dp_count, expert_count, capacity)
    summed = lax.psum_scatter(partial_value, "dp", scatter_dimension=0, tiled=True)
    returned = lax.all_to_all(summed, "expert", split_axis=1, concat_axis=1, tiled=True)[0]
    route_value = returned.reshape(-1)[slot_place].reshape(tok_count, route_count)
    own_values = jnp.dot(own_tokens.astype(jnp.float32), value_weight, precision=highest) + jnp.sum(
        route_prob * route_value, axis=1
    )
    segment = segment_ids[0]
    marker = passed_along(segment[:1] + 1, "expert", -1)
    carries = marker[0] == segment[-1] + 1
    following = jnp.concatenate([segment[1:], jnp.where(carries, segment[-1:], -1)])
    ending = following != segment
    segment_hit = segment[:, None] == jnp.arange(scores.shape[1], dtype=jnp.int32)[None, :]
    score_pick = jnp.sum(jnp.where(segment_hit, scores[0][None, :], 0.0), axis=1)
    reward = penalty_reward[0] + jnp.where(ending, score_pick, 0.0)
    position = jnp.arange(tok_count, dtype=jnp.int32)
    offset = (position[None, :] - position[:, None]).astype(jnp.float32)
    log_rate = jnp.log(jnp.float32(discount_rate))
    same_segment = (segment[:, None] == segment[None, :]) & (offset >= 0.0)
    discount = jnp.where(same_segment, jnp.exp(offset * log_rate), 0.0)
    local_return = jnp.dot(discount, reward, precision=highest)
    reach = jnp.where(
        (segment == segment[-1]) & carries,
        jnp.exp((tok_count - position).astype(jnp.float32) * log_rate),
        0.0,
    )
    identity = (jnp.ones((), jnp.float32), jnp.zeros((), jnp.float32))
    carry_in = entering((reach[0], local_return[0]), "expert", compose, identity)[1]
    returns = local_return + reach * carry_in
    mask_float = loss_mask[0].astype(jnp.float32)
    token_total, return_total = lax.psum(
        (jnp.sum(mask_float), jnp.sum(mask_float * returns)), ("dp", "expert")
    )
    divisor = jnp.maximum(token_total, 1.0)
    centre = return_total / divisor
    deviation = returns - centre
    spread_total = lax.psum(jnp.sum(mask_float * deviation * deviation), ("dp", "expert"))
    variance = spread_total / divisor
    whitened = (returns - centre) * lax.rsqrt(variance + white_epsilon)
    value_error = mask_float * (own_values - whitened)
    loss_part = 0.5 * jnp.sum(mask_float * (own_values - whitened) * (own_values - whitened))
    route_weight = value_error[:, None] * route_prob
    prob_grad = value_error[:, None] * route_value
    weight_table = (
        jnp.zeros((experts * capacity,), jnp.float32)
        .at[slot_place]
        .set(route_weight.reshape(-1))
        .reshape(experts, capacity)
    )
    owner_weight = lax.all_to_all(weight_table, "expert", split_axis=0, concat_axis=0, tiled=True)
    owner_weight = lax.all_gather(owner_weight[None], "dp", axis=0, tiled=True)
    row_weight = owner_weight.reshape(-1)
    spread = jnp.dot(row_weight, hidden.astype(jnp.float32), precision=highest)
    down_grad = (spread[:, None] * value_weight[None, :]).astype(jnp.bfloat16)
    hidden_grad = row_weight[:, None] * value_along[None, :]
    gate_delta = (hidden_grad * up_value * gate_sig * (1.0 + gate_value * (1.0 - gate_sig))).astype(
        jnp.bfloat16
    )
    up_delta = (hidden_grad * gate_value * gate_sig).astype(jnp.bfloat16)
    both_delta = jnp.concatenate([gate_delta, up_delta], axis=1)
    both_grad = lax.dot_general(
        both_delta, expert_rows, first_first, preferred_element_type=jnp.float32
    ).astype(jnp.bfloat16)
    gate_grad = both_grad[:hidden_width]
    up_grad = both_grad[hidden_width:]
    sigma_grad = (
        prob_grad - jnp.sum(prob_grad * route_prob, axis=1, keepdims=True)
    ) / sigmoid_total
    chosen_grad = sigma_grad * gate_sigmoid * (1.0 - gate_sigmoid)
    expert_hit = own_routes[:, :, None] == jnp.arange(experts, dtype=jnp.int32)[None, None, :]
    logit_grad = jnp.sum(jnp.where(expert_hit, chosen_grad[:, :, None], 0.0), axis=1)
    router_part = lax.dot_general(
        logit_grad, normed.astype(jnp.float32), first_first, precision=highest
    )
    value_part = jnp.dot(value_error, own_tokens.astype(jnp.float32), precision=highest) + jnp.dot(
        spread, down_float, precision=highest
    )
    router_grad, value_grad, loss_total = lax.psum(
        (router_part, value_part, loss_part), ("dp", "expert")
    )
    mean_loss = loss_total / divisor
    return (
        own_values[None],
        mean_loss,
        value_grad,
        router_grad,
        gate_grad[None],
        up_grad[None],
        down_grad[None],
    )


def solution(mesh):
    placed = (
        P("dp", "expert", None),
        P(),
        P(),
        P(),
        P("expert", "dp", None),
        P("expert", "dp", None),
        P("expert", "dp", None),
        P("dp", "expert", None),
        P("dp", "expert"),
        P("dp", "expert"),
        P("dp", "expert"),
        P("dp", None),
    )
    return jax.shard_map(
        shards,
        mesh=mesh,
        in_specs=placed,
        out_specs=(
            P("dp", "expert"),
            P(),
            P(),
            P(),
            P("expert", "dp", None),
            P("expert", "dp", None),
            P("expert", "dp", None),
        ),
        check_vma=False,
    )
```

```python
import functools

import jax
import jax.numpy as jnp
from jax import lax
from jax.sharding import PartitionSpec as P

discount_rate = 0.9995
norm_epsilon = 1e-06
white_epsilon = 1e-05
highest = lax.Precision.HIGHEST


def norm_rows(tokens, norm_gain):
    as_float = tokens.astype(jnp.float32)
    inverse_rms = lax.rsqrt(jnp.mean(as_float * as_float, axis=-1, keepdims=True) + norm_epsilon)
    return (as_float * inverse_rms * norm_gain).astype(jnp.bfloat16)


def slot_numbers(block_routes, experts):
    flattened = block_routes.reshape(-1)
    place = jnp.arange(flattened.shape[0], dtype=jnp.int32)
    same = (flattened[:, None] == flattened[None, :]) & (place[None, :] < place[:, None])
    return jnp.sum(same.astype(jnp.int32), axis=1).reshape(block_routes.shape)


def shifted_back(array, by, fill):
    return jnp.concatenate(
        [array[:, by:], jnp.full((array.shape[0], by), fill, array.dtype)], axis=1
    )


def row_returns(reward, same_next):
    total, factor, by = reward, discount_rate * same_next, 1
    while by < reward.shape[1]:
        total = total + factor * shifted_back(total, by, 0.0)
        factor = factor * shifted_back(factor, by, 0.0)
        by *= 2
    return total


def expert_block(outgoing):
    incoming = lax.all_to_all(outgoing, "expert", split_axis=0, concat_axis=0, tiled=True)
    return lax.all_gather(incoming[None], "dp", axis=0, tiled=True)


def shards(
    tokens,
    norm_gain,
    router_weight,
    value_weight,
    gate_weight,
    up_weight,
    down_weight,
    routes,
    segment_ids,
    loss_mask,
    penalty_reward,
    scores,
):
    tok_count = tokens.shape[1]
    model_width = tokens.shape[2]
    route_count = routes.shape[2]
    experts = router_weight.shape[0]
    dp_count = lax.axis_size("dp")
    expert_count = lax.axis_size("expert")
    devices = dp_count * expert_count
    both = ("dp", "expert")
    me = lax.axis_index("dp") * expert_count + lax.axis_index("expert")
    capacity = tok_count * route_count * 3 // (2 * experts)
    last_last = (((1,), (1,)), ((), ()))
    first_first = (((0,), (0,)), ((), ()))
    own_tokens = tokens[0]
    own_routes = routes[0]
    mask_float = loss_mask[0].astype(jnp.float32)

    segment = segment_ids[0]
    segment_hit = segment[:, None] == jnp.arange(scores.shape[1], dtype=jnp.int32)[None, :]
    score_pick = jnp.sum(jnp.where(segment_hit, scores[0][None, :], 0.0), axis=1)
    small = jnp.stack([segment.astype(jnp.float32), mask_float, penalty_reward[0], score_pick])
    small = lax.all_gather(small, both, axis=0, tiled=False)
    small = jnp.transpose(small, (1, 0, 2)).reshape(4, dp_count, expert_count * tok_count)

    normed = norm_rows(own_tokens, norm_gain)
    slot_number = slot_numbers(own_routes, experts)
    slot_place = own_routes * capacity + slot_number
    slots = jnp.arange(experts * capacity, dtype=jnp.int32)
    hits = [slots[:, None] == slot_place[:, k][None, :] for k in range(route_count)]
    pick = functools.reduce(jnp.logical_or, hits).astype(jnp.bfloat16)
    outgoing = jnp.dot(pick, normed, preferred_element_type=jnp.float32).astype(jnp.bfloat16)
    outgoing = outgoing.reshape(experts, capacity, model_width)
    expert_rows = expert_block(outgoing).reshape(-1, model_width)

    normed_float = normed.astype(jnp.float32)
    logits = lax.dot_general(normed_float, router_weight, last_last, precision=highest)
    expert_hit = own_routes[:, :, None] == jnp.arange(experts, dtype=jnp.int32)[None, None, :]
    chosen = jnp.sum(jnp.where(expert_hit, logits[:, None, :], 0.0), axis=2)
    gate_sigmoid = jax.nn.sigmoid(chosen)
    sigmoid_total = jnp.sum(gate_sigmoid, axis=1, keepdims=True)
    route_prob = gate_sigmoid / sigmoid_total

    segments, masks, penalties, picks = small
    same_next = (shifted_back(segments, 1, -1.0) == segments).astype(jnp.float32)
    returns = row_returns(penalties + jnp.where(same_next > 0.0, 0.0, picks), same_next)
    divisor = jnp.maximum(jnp.sum(masks), 1.0)
    centre = jnp.sum(masks * returns) / divisor
    deviation = returns - centre
    variance = jnp.sum(masks * deviation * deviation) / divisor
    whitened = deviation * lax.rsqrt(variance + white_epsilon)
    whitened = lax.dynamic_index_in_dim(whitened.reshape(devices, tok_count), me, 0, False)

    down_float = down_weight[0].astype(jnp.float32)
    value_along = jnp.dot(down_float, value_weight, precision=highest)
    own_head = jnp.dot(own_tokens.astype(jnp.float32), value_weight, precision=highest)

    gate_value = lax.dot_general(
        expert_rows, gate_weight[0], last_last, preferred_element_type=jnp.float32
    )
    up_value = lax.dot_general(
        expert_rows, up_weight[0], last_last, preferred_element_type=jnp.float32
    )
    gate_sig = jax.nn.sigmoid(gate_value)
    hidden = (gate_value * gate_sig * up_value).astype(jnp.bfloat16)
    partial_value = jnp.sum(hidden.astype(jnp.float32) * value_along[None, :], axis=1)
    returned = lax.all_to_all(
        partial_value.reshape(devices, capacity), both, split_axis=0, concat_axis=0, tiled=True
    )
    returned = jnp.sum(returned.reshape(dp_count, expert_count * capacity), axis=0)
    route_value = jnp.stack(
        [jnp.sum(jnp.where(hit, returned[:, None], 0.0), axis=0) for hit in hits], axis=1
    )
    own_values = own_head + jnp.sum(route_prob * route_value, axis=1)
    value_error = mask_float * (own_values - whitened)
    loss_part = 0.5 * jnp.sum(mask_float * (own_values - whitened) * (own_values - whitened))
    route_weight = value_error[:, None] * route_prob
    prob_grad = value_error[:, None] * route_value
    weight_table = sum(
        jnp.sum(jnp.where(hit, route_weight[:, k][None, :], 0.0), axis=1)
        for k, hit in enumerate(hits)
    ).reshape(1, experts, capacity)
    weight_table = jnp.broadcast_to(weight_table, (dp_count, experts, capacity))
    row_weight = lax.all_to_all(
        weight_table.reshape(devices, capacity), both, split_axis=0, concat_axis=0, tiled=True
    ).reshape(-1)
    spread = jnp.sum(row_weight[:, None] * hidden.astype(jnp.float32), axis=0)
    down_grad = (spread[:, None] * value_weight[None, :]).astype(jnp.bfloat16)
    hidden_grad = row_weight[:, None] * value_along[None, :]
    gate_delta = (hidden_grad * up_value * gate_sig * (1.0 + gate_value * (1.0 - gate_sig))).astype(
        jnp.bfloat16
    )
    up_delta = (hidden_grad * gate_value * gate_sig).astype(jnp.bfloat16)
    sigma_grad = (
        prob_grad - jnp.sum(prob_grad * route_prob, axis=1, keepdims=True)
    ) / sigmoid_total
    chosen_grad = sigma_grad * gate_sigmoid * (1.0 - gate_sigmoid)
    logit_grad = jnp.sum(jnp.where(expert_hit, chosen_grad[:, :, None], 0.0), axis=1)
    router_part = lax.dot_general(logit_grad, normed_float, first_first, precision=highest)
    value_part = jnp.dot(value_error, own_tokens.astype(jnp.float32), precision=highest) + jnp.dot(
        spread, down_float, precision=highest
    )
    parts = jnp.concatenate(
        [router_part, value_part[None], jnp.full((1, model_width), loss_part)], axis=0
    )
    parts = jnp.transpose(parts.reshape(experts + 2, devices, -1), (1, 0, 2))
    parts = lax.all_to_all(parts, both, split_axis=0, concat_axis=0, tiled=True)
    totals = lax.all_gather(jnp.sum(parts, axis=0), both, axis=0, tiled=False)
    totals = jnp.transpose(totals, (1, 0, 2)).reshape(experts + 2, model_width)
    gate_grad = lax.dot_general(
        gate_delta, expert_rows, first_first, preferred_element_type=jnp.float32
    ).astype(jnp.bfloat16)
    up_grad = lax.dot_general(
        up_delta, expert_rows, first_first, preferred_element_type=jnp.float32
    ).astype(jnp.bfloat16)
    return (
        own_values[None],
        totals[experts + 1, 0] / divisor,
        totals[experts],
        totals[:experts],
        gate_grad[None],
        up_grad[None],
        down_grad[None],
    )


def solution(mesh):
    placed = (
        P("dp", "expert", None),
        P(),
        P(),
        P(),
        P("expert", "dp", None),
        P("expert", "dp", None),
        P("expert", "dp", None),
        P("dp", "expert", None),
        P("dp", "expert"),
        P("dp", "expert"),
        P("dp", "expert"),
        P("dp", None),
    )
    return jax.shard_map(
        shards,
        mesh=mesh,
        in_specs=placed,
        out_specs=(
            P("dp", "expert"),
            P(),
            P(),
            P(),
            P("expert", "dp", None),
            P("expert", "dp", None),
            P("expert", "dp", None),
        ),
        check_vma=False,
    )
```

```python
import functools

import jax
import jax.numpy as jnp
from jax import lax
from jax.sharding import PartitionSpec as P

discount_rate = 0.9995
norm_epsilon = 1e-06
white_epsilon = 1e-05
highest = lax.Precision.HIGHEST


def norm_rows(tokens, norm_gain):
    as_float = tokens.astype(jnp.float32)
    inverse_rms = lax.rsqrt(jnp.mean(as_float * as_float, axis=-1, keepdims=True) + norm_epsilon)
    return (as_float * inverse_rms * norm_gain).astype(jnp.bfloat16)


def slot_numbers(block_routes, experts):
    flattened = block_routes.reshape(-1)
    place = jnp.arange(flattened.shape[0], dtype=jnp.int32)
    same = (flattened[:, None] == flattened[None, :]) & (place[None, :] < place[:, None])
    return jnp.sum(same.astype(jnp.int32), axis=1).reshape(block_routes.shape)


def shifted_back(array, by, fill):
    return jnp.concatenate(
        [array[:, by:], jnp.full((array.shape[0], by), fill, array.dtype)], axis=1
    )


def row_returns(reward, same_next):
    total, factor, by = reward, discount_rate * same_next, 1
    while by < reward.shape[1]:
        total = total + factor * shifted_back(total, by, 0.0)
        factor = factor * shifted_back(factor, by, 0.0)
        by *= 2
    return total


def to_all(array, axes):
    count = lax.axis_size(axes[0]) * lax.axis_size(axes[1])
    copies = jnp.broadcast_to(array[None], (count, *array.shape))
    return lax.all_to_all(copies, axes, split_axis=0, concat_axis=0, tiled=True)


def expert_block(outgoing):
    incoming = lax.all_to_all(outgoing, "expert", split_axis=0, concat_axis=0, tiled=True)
    return lax.all_gather(incoming[None], "dp", axis=0, tiled=True)


def shards(
    tokens,
    norm_gain,
    router_weight,
    value_weight,
    gate_weight,
    up_weight,
    down_weight,
    routes,
    segment_ids,
    loss_mask,
    penalty_reward,
    scores,
):
    tok_count = tokens.shape[1]
    model_width = tokens.shape[2]
    route_count = routes.shape[2]
    experts = router_weight.shape[0]
    dp_count = lax.axis_size("dp")
    expert_count = lax.axis_size("expert")
    devices = dp_count * expert_count
    both = ("dp", "expert")
    me = lax.axis_index("dp") * expert_count + lax.axis_index("expert")
    capacity = tok_count * route_count * 3 // (2 * experts)
    last_last = (((1,), (1,)), ((), ()))
    first_first = (((0,), (0,)), ((), ()))
    own_tokens = tokens[0]
    own_routes = routes[0]
    mask_float = loss_mask[0].astype(jnp.float32)

    segment = segment_ids[0]
    segment_hit = segment[:, None] == jnp.arange(scores.shape[1], dtype=jnp.int32)[None, :]
    score_pick = jnp.sum(jnp.where(segment_hit, scores[0][None, :], 0.0), axis=1)
    small = jnp.stack([segment.astype(jnp.float32), mask_float, penalty_reward[0], score_pick])
    small = to_all(small, both)
    small = jnp.transpose(small, (1, 0, 2)).reshape(4, dp_count, expert_count * tok_count)

    normed = norm_rows(own_tokens, norm_gain)
    slot_number = slot_numbers(own_routes, experts)
    slot_place = own_routes * capacity + slot_number
    slots = jnp.arange(experts * capacity, dtype=jnp.int32)
    hits = [slots[:, None] == slot_place[:, k][None, :] for k in range(route_count)]
    pick = functools.reduce(jnp.logical_or, hits).astype(jnp.bfloat16)
    outgoing = jnp.dot(pick, normed, preferred_element_type=jnp.float32).astype(jnp.bfloat16)
    outgoing = outgoing.reshape(experts, capacity, model_width)
    chunks = max(capacity // 16, 1)
    chunk = capacity // chunks
    row_chunks = [
        expert_block(outgoing[:, c * chunk : (c + 1) * chunk]).reshape(-1, model_width)
        for c in range(chunks)
    ]

    normed_float = normed.astype(jnp.float32)
    logits = lax.dot_general(normed_float, router_weight, last_last, precision=highest)
    expert_hit = own_routes[:, :, None] == jnp.arange(experts, dtype=jnp.int32)[None, None, :]
    chosen = jnp.sum(jnp.where(expert_hit, logits[:, None, :], 0.0), axis=2)
    gate_sigmoid = jax.nn.sigmoid(chosen)
    sigmoid_total = jnp.sum(gate_sigmoid, axis=1, keepdims=True)
    route_prob = gate_sigmoid / sigmoid_total

    segments, masks, penalties, picks = small
    same_next = (shifted_back(segments, 1, -1.0) == segments).astype(jnp.float32)
    returns = row_returns(penalties + jnp.where(same_next > 0.0, 0.0, picks), same_next)
    divisor = jnp.maximum(jnp.sum(masks), 1.0)
    centre = jnp.sum(masks * returns) / divisor
    deviation = returns - centre
    variance = jnp.sum(masks * deviation * deviation) / divisor
    whitened = deviation * lax.rsqrt(variance + white_epsilon)
    whitened = lax.dynamic_index_in_dim(whitened.reshape(devices, tok_count), me, 0, False)

    down_float = down_weight[0].astype(jnp.float32)
    value_along = jnp.dot(down_float, value_weight, precision=highest)
    own_head = jnp.dot(own_tokens.astype(jnp.float32), value_weight, precision=highest)

    kept, partial_values = [], []
    for rows in row_chunks:
        gate_value = lax.dot_general(
            rows, gate_weight[0], last_last, preferred_element_type=jnp.float32
        )
        up_value = lax.dot_general(
            rows, up_weight[0], last_last, preferred_element_type=jnp.float32
        )
        gate_sig = jax.nn.sigmoid(gate_value)
        hidden = (gate_value * gate_sig * up_value).astype(jnp.bfloat16)
        partial = jnp.sum(hidden.astype(jnp.float32) * value_along[None, :], axis=1)
        partial_values.append(partial.reshape(devices, chunk))
        kept.append((gate_value, up_value, gate_sig, hidden))
    partial_value = jnp.concatenate(partial_values, axis=1)
    returned = lax.all_to_all(
        partial_value, both, split_axis=0, concat_axis=0, tiled=True
    )
    returned = jnp.sum(returned.reshape(dp_count, expert_count * capacity), axis=0)
    route_value = jnp.stack(
        [jnp.sum(jnp.where(hit, returned[:, None], 0.0), axis=0) for hit in hits], axis=1
    )
    own_values = own_head + jnp.sum(route_prob * route_value, axis=1)
    value_error = mask_float * (own_values - whitened)
    loss_part = 0.5 * jnp.sum(mask_float * (own_values - whitened) * (own_values - whitened))
    route_weight = value_error[:, None] * route_prob
    prob_grad = value_error[:, None] * route_value
    weight_table = sum(
        jnp.sum(jnp.where(hit, route_weight[:, k][None, :], 0.0), axis=1)
        for k, hit in enumerate(hits)
    ).reshape(1, experts, capacity)
    weight_table = jnp.broadcast_to(weight_table, (dp_count, experts, capacity))
    row_weight = lax.all_to_all(
        weight_table.reshape(devices, capacity), both, split_axis=0, concat_axis=0, tiled=True
    )
    spread, gate_deltas, up_deltas = 0.0, [], []
    for c, (gate_value, up_value, gate_sig, hidden) in enumerate(kept):
        weights = row_weight[:, c * chunk : (c + 1) * chunk].reshape(-1)
        spread = spread + jnp.sum(weights[:, None] * hidden.astype(jnp.float32), axis=0)
        hidden_grad = weights[:, None] * value_along[None, :]
        gate_deltas.append(
            (hidden_grad * up_value * gate_sig * (1.0 + gate_value * (1.0 - gate_sig))).astype(
                jnp.bfloat16
            )
        )
        up_deltas.append((hidden_grad * gate_value * gate_sig).astype(jnp.bfloat16))
    down_grad = (spread[:, None] * value_weight[None, :]).astype(jnp.bfloat16)
    sigma_grad = (
        prob_grad - jnp.sum(prob_grad * route_prob, axis=1, keepdims=True)
    ) / sigmoid_total
    chosen_grad = sigma_grad * gate_sigmoid * (1.0 - gate_sigmoid)
    logit_grad = jnp.sum(jnp.where(expert_hit, chosen_grad[:, :, None], 0.0), axis=1)
    router_part = lax.dot_general(logit_grad, normed_float, first_first, precision=highest)
    value_part = jnp.dot(value_error, own_tokens.astype(jnp.float32), precision=highest) + jnp.dot(
        spread, down_float, precision=highest
    )
    parts = jnp.concatenate(
        [router_part, value_part[None], jnp.full((1, model_width), loss_part)], axis=0
    )
    parts = jnp.transpose(parts.reshape(experts + 2, devices, -1), (1, 0, 2))
    parts = lax.all_to_all(parts, both, split_axis=0, concat_axis=0, tiled=True)
    totals = to_all(jnp.sum(parts, axis=0), both)
    totals = jnp.transpose(totals, (1, 0, 2)).reshape(experts + 2, model_width)
    gate_grad, up_grad = [
        sum(
            lax.dot_general(delta, rows, first_first, preferred_element_type=jnp.float32)
            for delta, rows in zip(deltas, row_chunks)
        ).astype(jnp.bfloat16)
        for deltas in (gate_deltas, up_deltas)
    ]
    return (
        own_values[None],
        totals[experts + 1, 0] / divisor,
        totals[experts],
        totals[:experts],
        gate_grad[None],
        up_grad[None],
        down_grad[None],
    )


def solution(mesh):
    placed = (
        P("dp", "expert", None),
        P(),
        P(),
        P(),
        P("expert", "dp", None),
        P("expert", "dp", None),
        P("expert", "dp", None),
        P("dp", "expert", None),
        P("dp", "expert"),
        P("dp", "expert"),
        P("dp", "expert"),
        P("dp", None),
    )
    return jax.shard_map(
        shards,
        mesh=mesh,
        in_specs=placed,
        out_specs=(
            P("dp", "expert"),
            P(),
            P(),
            P(),
            P("expert", "dp", None),
            P("expert", "dp", None),
            P("expert", "dp", None),
        ),
        check_vma=False,
    )
```

```python
import functools

import jax
import jax.numpy as jnp
from jax import lax
from jax.sharding import PartitionSpec as P

discount_rate = 0.9995
norm_epsilon = 1e-06
white_epsilon = 1e-05
highest = lax.Precision.HIGHEST


def norm_rows(tokens, norm_gain):
    as_float = tokens.astype(jnp.float32)
    inverse_rms = lax.rsqrt(jnp.mean(as_float * as_float, axis=-1, keepdims=True) + norm_epsilon)
    return (as_float * inverse_rms * norm_gain).astype(jnp.bfloat16)


def slot_numbers(block_routes, experts):
    flattened = block_routes.reshape(-1)
    place = jnp.arange(flattened.shape[0], dtype=jnp.int32)
    same = (flattened[:, None] == flattened[None, :]) & (place[None, :] < place[:, None])
    return jnp.sum(same.astype(jnp.int32), axis=1).reshape(block_routes.shape)


def shifted_back(array, by, fill):
    return jnp.concatenate(
        [array[:, by:], jnp.full((array.shape[0], by), fill, array.dtype)], axis=1
    )


def row_returns(reward, same_next):
    total, factor, by = reward, discount_rate * same_next, 1
    while by < reward.shape[1]:
        total = total + factor * shifted_back(total, by, 0.0)
        factor = factor * shifted_back(factor, by, 0.0)
        by *= 2
    return total


def to_all(array, axes):
    count = lax.axis_size(axes[0]) * lax.axis_size(axes[1])
    copies = jnp.broadcast_to(array[None], (count, *array.shape))
    return lax.all_to_all(copies, axes, split_axis=0, concat_axis=0, tiled=True)


def across_dp(block):
    count = lax.axis_size("dp")
    blocks, bits = {0: block}, count // 2
    while bits:
        pairs = [(i, i ^ bits) for i in range(count)]
        blocks |= {k ^ bits: lax.ppermute(held, "dp", pairs) for k, held in blocks.items()}
        bits //= 2
    return jnp.stack([blocks[k] for k in range(count)])


def expert_block(outgoing):
    incoming = lax.all_to_all(outgoing, "expert", split_axis=0, concat_axis=0, tiled=True)
    count = lax.axis_size("dp")
    if count & (count - 1):
        return lax.all_gather(incoming, "dp", axis=0)
    return across_dp(incoming)


def reordered(table, count, own):
    if count & (count - 1):
        return table
    turned = jnp.arange(count, dtype=jnp.int32) ^ own
    hit = turned[:, None] == jnp.arange(count, dtype=jnp.int32)[None, :]
    hit = hit.reshape(count, count, *(1,) * (table.ndim - 1))
    return jnp.sum(jnp.where(hit, table[None], 0.0), axis=1)


def shards(
    tokens,
    norm_gain,
    router_weight,
    value_weight,
    gate_weight,
    up_weight,
    down_weight,
    routes,
    segment_ids,
    loss_mask,
    penalty_reward,
    scores,
):
    tok_count = tokens.shape[1]
    model_width = tokens.shape[2]
    route_count = routes.shape[2]
    experts = router_weight.shape[0]
    dp_count = lax.axis_size("dp")
    expert_count = lax.axis_size("expert")
    devices = dp_count * expert_count
    both = ("dp", "expert")
    me = lax.axis_index("dp") * expert_count + lax.axis_index("expert")
    capacity = tok_count * route_count * 3 // (2 * experts)
    last_last = (((1,), (1,)), ((), ()))
    first_first = (((0,), (0,)), ((), ()))
    own_tokens = tokens[0]
    own_routes = routes[0]
    mask_float = loss_mask[0].astype(jnp.float32)

    segment = segment_ids[0]
    segment_hit = segment[:, None] == jnp.arange(scores.shape[1], dtype=jnp.int32)[None, :]
    score_pick = jnp.sum(jnp.where(segment_hit, scores[0][None, :], 0.0), axis=1)
    small = jnp.stack([segment.astype(jnp.float32), mask_float, penalty_reward[0], score_pick])
    small = to_all(small, both)
    small = jnp.transpose(small, (1, 0, 2)).reshape(4, dp_count, expert_count * tok_count)

    normed = norm_rows(own_tokens, norm_gain)
    slot_number = slot_numbers(own_routes, experts)
    slot_place = own_routes * capacity + slot_number
    slots = jnp.arange(experts * capacity, dtype=jnp.int32)
    hits = [slots[:, None] == slot_place[:, k][None, :] for k in range(route_count)]
    pick = functools.reduce(jnp.logical_or, hits).astype(jnp.bfloat16)
    outgoing = jnp.dot(pick, normed, preferred_element_type=jnp.float32).astype(jnp.bfloat16)
    outgoing = outgoing.reshape(experts, capacity, model_width)
    chunks = max(capacity // 16, 1)
    chunk = capacity // chunks
    row_chunks = [
        expert_block(outgoing[:, c * chunk : (c + 1) * chunk]).reshape(-1, model_width)
        for c in range(chunks)
    ]

    normed_float = normed.astype(jnp.float32)
    logits = lax.dot_general(normed_float, router_weight, last_last, precision=highest)
    expert_hit = own_routes[:, :, None] == jnp.arange(experts, dtype=jnp.int32)[None, None, :]
    chosen = jnp.sum(jnp.where(expert_hit, logits[:, None, :], 0.0), axis=2)
    gate_sigmoid = jax.nn.sigmoid(chosen)
    sigmoid_total = jnp.sum(gate_sigmoid, axis=1, keepdims=True)
    route_prob = gate_sigmoid / sigmoid_total

    segments, masks, penalties, picks = small
    same_next = (shifted_back(segments, 1, -1.0) == segments).astype(jnp.float32)
    returns = row_returns(penalties + jnp.where(same_next > 0.0, 0.0, picks), same_next)
    divisor = jnp.maximum(jnp.sum(masks), 1.0)
    centre = jnp.sum(masks * returns) / divisor
    deviation = returns - centre
    variance = jnp.sum(masks * deviation * deviation) / divisor
    whitened = deviation * lax.rsqrt(variance + white_epsilon)
    whitened = lax.dynamic_index_in_dim(whitened.reshape(devices, tok_count), me, 0, False)

    down_float = down_weight[0].astype(jnp.float32)
    value_along = jnp.dot(down_float, value_weight, precision=highest)
    own_head = jnp.dot(own_tokens.astype(jnp.float32), value_weight, precision=highest)

    kept, partial_values = [], []
    for rows in row_chunks:
        gate_value = lax.dot_general(
            rows, gate_weight[0], last_last, preferred_element_type=jnp.float32
        )
        up_value = lax.dot_general(
            rows, up_weight[0], last_last, preferred_element_type=jnp.float32
        )
        gate_sig = jax.nn.sigmoid(gate_value)
        hidden = (gate_value * gate_sig * up_value).astype(jnp.bfloat16)
        partial = jnp.sum(hidden.astype(jnp.float32) * value_along[None, :], axis=1)
        partial_values.append(partial.reshape(dp_count, expert_count, chunk))
        gate_slope = value_along * up_value * gate_sig * (1.0 + gate_value * (1.0 - gate_sig))
        up_slope = value_along * gate_value * gate_sig
        kept.append((rows, hidden, gate_slope, up_slope))
    expert_rows, hidden, gate_slope, up_slope = [jnp.concatenate(a, axis=0) for a in zip(*kept)]
    partial_value = reordered(
        jnp.concatenate(partial_values, axis=2), dp_count, lax.axis_index("dp")
    ).reshape(devices, capacity)
    returned = lax.all_to_all(
        partial_value, both, split_axis=0, concat_axis=0, tiled=True
    )
    returned = jnp.sum(returned.reshape(dp_count, expert_count * capacity), axis=0)
    route_value = jnp.stack(
        [jnp.sum(jnp.where(hit, returned[:, None], 0.0), axis=0) for hit in hits], axis=1
    )
    own_values = own_head + jnp.sum(route_prob * route_value, axis=1)
    value_error = mask_float * (own_values - whitened)
    loss_part = 0.5 * jnp.sum(mask_float * (own_values - whitened) * (own_values - whitened))
    route_weight = value_error[:, None] * route_prob
    prob_grad = value_error[:, None] * route_value
    weight_table = sum(
        jnp.sum(jnp.where(hit, route_weight[:, k][None, :], 0.0), axis=1)
        for k, hit in enumerate(hits)
    ).reshape(1, experts, capacity)
    weight_table = jnp.broadcast_to(weight_table, (dp_count, experts, capacity))
    row_weight = lax.all_to_all(
        weight_table.reshape(devices, capacity), both, split_axis=0, concat_axis=0, tiled=True
    )
    row_weight = reordered(
        row_weight.reshape(dp_count, expert_count, capacity), dp_count, lax.axis_index("dp")
    ).reshape(dp_count, expert_count, chunks, chunk)
    row_weight = jnp.transpose(row_weight, (2, 0, 1, 3)).reshape(-1)
    spread = jnp.sum(row_weight[:, None] * hidden.astype(jnp.float32), axis=0)
    gate_delta = (row_weight[:, None] * gate_slope).astype(jnp.bfloat16)
    up_delta = (row_weight[:, None] * up_slope).astype(jnp.bfloat16)
    down_grad = (spread[:, None] * value_weight[None, :]).astype(jnp.bfloat16)
    sigma_grad = (
        prob_grad - jnp.sum(prob_grad * route_prob, axis=1, keepdims=True)
    ) / sigmoid_total
    chosen_grad = sigma_grad * gate_sigmoid * (1.0 - gate_sigmoid)
    logit_grad = jnp.sum(jnp.where(expert_hit, chosen_grad[:, :, None], 0.0), axis=1)
    router_part = lax.dot_general(logit_grad, normed_float, first_first, precision=highest)
    value_part = jnp.dot(value_error, own_tokens.astype(jnp.float32), precision=highest) + jnp.dot(
        spread, down_float, precision=highest
    )
    parts = jnp.concatenate(
        [router_part, value_part[None], jnp.full((1, model_width), loss_part)], axis=0
    )
    parts = jnp.transpose(parts.reshape(experts + 2, devices, -1), (1, 0, 2))
    parts = lax.all_to_all(parts, both, split_axis=0, concat_axis=0, tiled=True)
    totals = to_all(jnp.sum(parts, axis=0), both)
    totals = jnp.transpose(totals, (1, 0, 2)).reshape(experts + 2, model_width)
    gate_grad, up_grad = [
        lax.dot_general(
            delta, expert_rows, first_first, preferred_element_type=jnp.float32
        ).astype(jnp.bfloat16)
        for delta in (gate_delta, up_delta)
    ]
    return (
        own_values[None],
        totals[experts + 1, 0] / divisor,
        totals[experts],
        totals[:experts],
        gate_grad[None],
        up_grad[None],
        down_grad[None],
    )


def solution(mesh):
    placed = (
        P("dp", "expert", None),
        P(),
        P(),
        P(),
        P("expert", "dp", None),
        P("expert", "dp", None),
        P("expert", "dp", None),
        P("dp", "expert", None),
        P("dp", "expert"),
        P("dp", "expert"),
        P("dp", "expert"),
        P("dp", None),
    )
    return jax.shard_map(
        shards,
        mesh=mesh,
        in_specs=placed,
        out_specs=(
            P("dp", "expert"),
            P(),
            P(),
            P(),
            P("expert", "dp", None),
            P("expert", "dp", None),
            P("expert", "dp", None),
        ),
        check_vma=False,
    )
```

```python
import functools

import jax
import jax.numpy as jnp
from jax import lax
from jax.sharding import PartitionSpec as P

discount_rate = 0.9995
norm_epsilon = 1e-06
white_epsilon = 1e-05
highest = lax.Precision.HIGHEST


def norm_rows(tokens, norm_gain):
    as_float = tokens.astype(jnp.float32)
    inverse_rms = lax.rsqrt(jnp.mean(as_float * as_float, axis=-1, keepdims=True) + norm_epsilon)
    return (as_float * inverse_rms * norm_gain).astype(jnp.bfloat16)


def slot_numbers(block_routes, experts):
    flattened = block_routes.reshape(-1)
    place = jnp.arange(flattened.shape[0], dtype=jnp.int32)
    same = (flattened[:, None] == flattened[None, :]) & (place[None, :] < place[:, None])
    return jnp.sum(same.astype(jnp.int32), axis=1).reshape(block_routes.shape)


def shifted_back(array, by, fill):
    return jnp.concatenate(
        [array[:, by:], jnp.full((array.shape[0], by), fill, array.dtype)], axis=1
    )


def row_returns(reward, same_next):
    total, factor, by = reward, discount_rate * same_next, 1
    while by < reward.shape[1]:
        total = total + factor * shifted_back(total, by, 0.0)
        factor = factor * shifted_back(factor, by, 0.0)
        by *= 2
    return total


def to_all(array, axes):
    count = lax.axis_size(axes[0]) * lax.axis_size(axes[1])
    copies = jnp.broadcast_to(array[None], (count, *array.shape))
    return lax.all_to_all(copies, axes, split_axis=0, concat_axis=0, tiled=True)


def across_bit(blocks, bits):
    count = lax.axis_size("dp")
    pairs = [(i, i ^ bits) for i in range(count)]
    return blocks | {k ^ bits: lax.ppermute(held, "dp", pairs) for k, held in blocks.items()}


def expert_chunks(outgoing, chunks):
    count = lax.axis_size("dp")
    chunk = outgoing.shape[1] // chunks
    parts = [outgoing[:, c * chunk : (c + 1) * chunk] for c in range(chunks)]
    held = []
    for c in range(chunks):
        part = parts[c]
        if c > 1 and not count & (count - 1):
            part, held[c - 2] = lax.optimization_barrier((part, held[c - 2]))
        incoming = lax.all_to_all(part, "expert", split_axis=0, concat_axis=0, tiled=True)
        if count & (count - 1):
            held.append(lax.all_gather(incoming, "dp", axis=0))
        else:
            held.append(across_bit({0: incoming}, count // 2) if count > 1 else {0: incoming})
    if count & (count - 1):
        return held
    stacked = []
    for blocks in held:
        bits = count // 4
        while bits:
            blocks, bits = across_bit(blocks, bits), bits // 2
        stacked.append(jnp.stack([blocks[k] for k in range(count)]))
    return stacked


def reordered(table, count, own):
    if count & (count - 1):
        return table
    turned = jnp.arange(count, dtype=jnp.int32) ^ own
    hit = turned[:, None] == jnp.arange(count, dtype=jnp.int32)[None, :]
    hit = hit.reshape(count, count, *(1,) * (table.ndim - 1))
    return jnp.sum(jnp.where(hit, table[None], 0.0), axis=1)


def shards(
    tokens,
    norm_gain,
    router_weight,
    value_weight,
    gate_weight,
    up_weight,
    down_weight,
    routes,
    segment_ids,
    loss_mask,
    penalty_reward,
    scores,
):
    tok_count = tokens.shape[1]
    model_width = tokens.shape[2]
    route_count = routes.shape[2]
    experts = router_weight.shape[0]
    dp_count = lax.axis_size("dp")
    expert_count = lax.axis_size("expert")
    devices = dp_count * expert_count
    both = ("dp", "expert")
    me = lax.axis_index("dp") * expert_count + lax.axis_index("expert")
    capacity = tok_count * route_count * 3 // (2 * experts)
    last_last = (((1,), (1,)), ((), ()))
    first_first = (((0,), (0,)), ((), ()))
    own_tokens = tokens[0]
    own_routes = routes[0]
    mask_float = loss_mask[0].astype(jnp.float32)

    segment = segment_ids[0]
    segment_hit = segment[:, None] == jnp.arange(scores.shape[1], dtype=jnp.int32)[None, :]
    score_pick = jnp.sum(jnp.where(segment_hit, scores[0][None, :], 0.0), axis=1)
    small = jnp.stack([segment.astype(jnp.float32), mask_float, penalty_reward[0], score_pick])
    small = to_all(small, both)
    small = jnp.transpose(small, (1, 0, 2)).reshape(4, dp_count, expert_count * tok_count)

    normed = norm_rows(own_tokens, norm_gain)
    slot_number = slot_numbers(own_routes, experts)
    slot_place = own_routes * capacity + slot_number
    slots = jnp.arange(experts * capacity, dtype=jnp.int32)
    hits = [slots[:, None] == slot_place[:, k][None, :] for k in range(route_count)]
    pick = functools.reduce(jnp.logical_or, hits).astype(jnp.bfloat16)
    outgoing = jnp.dot(pick, normed, preferred_element_type=jnp.float32).astype(jnp.bfloat16)
    outgoing = outgoing.reshape(experts, capacity, model_width)
    chunks = max(capacity // 16, 1)
    chunk = capacity // chunks
    row_chunks = [rows.reshape(-1, model_width) for rows in expert_chunks(outgoing, chunks)]

    normed_float = normed.astype(jnp.float32)
    logits = lax.dot_general(normed_float, router_weight, last_last, precision=highest)
    expert_hit = own_routes[:, :, None] == jnp.arange(experts, dtype=jnp.int32)[None, None, :]
    chosen = jnp.sum(jnp.where(expert_hit, logits[:, None, :], 0.0), axis=2)
    gate_sigmoid = jax.nn.sigmoid(chosen)
    sigmoid_total = jnp.sum(gate_sigmoid, axis=1, keepdims=True)
    route_prob = gate_sigmoid / sigmoid_total

    segments, masks, penalties, picks = small
    same_next = (shifted_back(segments, 1, -1.0) == segments).astype(jnp.float32)
    returns = row_returns(penalties + jnp.where(same_next > 0.0, 0.0, picks), same_next)
    divisor = jnp.maximum(jnp.sum(masks), 1.0)
    centre = jnp.sum(masks * returns) / divisor
    deviation = returns - centre
    variance = jnp.sum(masks * deviation * deviation) / divisor
    whitened = deviation * lax.rsqrt(variance + white_epsilon)
    whitened = lax.dynamic_index_in_dim(whitened.reshape(devices, tok_count), me, 0, False)

    down_float = down_weight[0].astype(jnp.float32)
    value_along = jnp.dot(down_float, value_weight, precision=highest)
    own_head = jnp.dot(own_tokens.astype(jnp.float32), value_weight, precision=highest)

    kept, partial_values = [], []
    for rows in row_chunks:
        gate_value = lax.dot_general(
            rows, gate_weight[0], last_last, preferred_element_type=jnp.float32
        )
        up_value = lax.dot_general(
            rows, up_weight[0], last_last, preferred_element_type=jnp.float32
        )
        gate_sig = jax.nn.sigmoid(gate_value)
        hidden = (gate_value * gate_sig * up_value).astype(jnp.bfloat16)
        partial = jnp.sum(hidden.astype(jnp.float32) * value_along[None, :], axis=1)
        partial_values.append(partial.reshape(dp_count, expert_count, chunk))
        gate_slope = value_along * up_value * gate_sig * (1.0 + gate_value * (1.0 - gate_sig))
        up_slope = value_along * gate_value * gate_sig
        kept.append((rows, hidden, gate_slope, up_slope))
    expert_rows, hidden, gate_slope, up_slope = [jnp.concatenate(a, axis=0) for a in zip(*kept)]
    partial_value = reordered(
        jnp.concatenate(partial_values, axis=2), dp_count, lax.axis_index("dp")
    ).reshape(devices, capacity)
    returned = lax.all_to_all(
        partial_value, both, split_axis=0, concat_axis=0, tiled=True
    )
    returned = jnp.sum(returned.reshape(dp_count, expert_count * capacity), axis=0)
    route_value = jnp.stack(
        [jnp.sum(jnp.where(hit, returned[:, None], 0.0), axis=0) for hit in hits], axis=1
    )
    own_values = own_head + jnp.sum(route_prob * route_value, axis=1)
    value_error = mask_float * (own_values - whitened)
    loss_part = 0.5 * jnp.sum(mask_float * (own_values - whitened) * (own_values - whitened))
    route_weight = value_error[:, None] * route_prob
    prob_grad = value_error[:, None] * route_value
    weight_table = sum(
        jnp.sum(jnp.where(hit, route_weight[:, k][None, :], 0.0), axis=1)
        for k, hit in enumerate(hits)
    ).reshape(1, experts, capacity)
    weight_table = jnp.broadcast_to(weight_table, (dp_count, experts, capacity))
    row_weight = lax.all_to_all(
        weight_table.reshape(devices, capacity), both, split_axis=0, concat_axis=0, tiled=True
    )
    row_weight = reordered(
        row_weight.reshape(dp_count, expert_count, capacity), dp_count, lax.axis_index("dp")
    ).reshape(dp_count, expert_count, chunks, chunk)
    row_weight = jnp.transpose(row_weight, (2, 0, 1, 3)).reshape(-1)
    spread = jnp.sum(row_weight[:, None] * hidden.astype(jnp.float32), axis=0)
    gate_delta = (row_weight[:, None] * gate_slope).astype(jnp.bfloat16)
    up_delta = (row_weight[:, None] * up_slope).astype(jnp.bfloat16)
    down_grad = (spread[:, None] * value_weight[None, :]).astype(jnp.bfloat16)
    sigma_grad = (
        prob_grad - jnp.sum(prob_grad * route_prob, axis=1, keepdims=True)
    ) / sigmoid_total
    chosen_grad = sigma_grad * gate_sigmoid * (1.0 - gate_sigmoid)
    logit_grad = jnp.sum(jnp.where(expert_hit, chosen_grad[:, :, None], 0.0), axis=1)
    router_part = lax.dot_general(logit_grad, normed_float, first_first, precision=highest)
    value_part = jnp.dot(value_error, own_tokens.astype(jnp.float32), precision=highest) + jnp.dot(
        spread, down_float, precision=highest
    )
    parts = jnp.concatenate(
        [router_part, value_part[None], jnp.full((1, model_width), loss_part)], axis=0
    )
    parts = jnp.transpose(parts.reshape(experts + 2, devices, -1), (1, 0, 2))
    parts = lax.all_to_all(parts, both, split_axis=0, concat_axis=0, tiled=True)
    totals = to_all(jnp.sum(parts, axis=0), both)
    totals = jnp.transpose(totals, (1, 0, 2)).reshape(experts + 2, model_width)
    gate_grad, up_grad = [
        lax.dot_general(
            delta, expert_rows, first_first, preferred_element_type=jnp.float32
        ).astype(jnp.bfloat16)
        for delta in (gate_delta, up_delta)
    ]
    return (
        own_values[None],
        totals[experts + 1, 0] / divisor,
        totals[experts],
        totals[:experts],
        gate_grad[None],
        up_grad[None],
        down_grad[None],
    )


def solution(mesh):
    placed = (
        P("dp", "expert", None),
        P(),
        P(),
        P(),
        P("expert", "dp", None),
        P("expert", "dp", None),
        P("expert", "dp", None),
        P("dp", "expert", None),
        P("dp", "expert"),
        P("dp", "expert"),
        P("dp", "expert"),
        P("dp", None),
    )
    return jax.shard_map(
        shards,
        mesh=mesh,
        in_specs=placed,
        out_specs=(
            P("dp", "expert"),
            P(),
            P(),
            P(),
            P("expert", "dp", None),
            P("expert", "dp", None),
            P("expert", "dp", None),
        ),
        check_vma=False,
    )
```
